32 devices in a mesh: dom: 8 (over z, x), section: 4 (over y, core).
Axes of the slice: x: 2, y: 2, z: 4, core: 2. Of those that a mesh axis runs over, the one named last changes fastest.
Arguments:
- node_latents: bfloat16 [4, 4, 8192, 128], P('section', None, 'dom'), may hold values from -6 to 6
- cotangent: bfloat16 [4, 8192, 128], P(None, 'dom'), may hold values from -6 to 6
- tile_weights: bfloat16 [64, 4, 128, 128], P('dom'), may hold values from -0.25 to 0.25
- tile_source: int32 [64, 4], P('dom'), may hold values from 0 to 11, as said below
- tile_count: int32 [64], P('dom'), may hold values from 2 to 4, as said below
- send_blocks: int32 [8, 2, 2], P('dom'), may hold values from 0 to 7, as said below
- w_message: bfloat16 [4, 128, 128], P('section'), may hold values from -0.5 to 0.5
- w_first: bfloat16 [4, 256, 128], P('section'), may hold values from -0.375 to 0.375
- bias_first: float32 [4, 128], P('section'), may hold values from -3 to 3
- w_second: bfloat16 [4, 128, 128], P('section'), may hold values from -0.5 to 0.5
- norm_gain: float32 [4, 128], P('section'), may hold values from 0.1 to 1.9
Outputs:
- grad_inputs: bfloat16 [4, 4, 8192, 128], P('section', None, 'dom')
- grad_message: float32 [4, 128, 128], P('section')
- grad_first: float32 [4, 256, 128], P('section')
- grad_bias: float32 [4, 128], P('section')
- grad_second: float32 [4, 128, 128], P('section')
- grad_gain: float32 [4, 128], P('section')
The draws below stay inside these ranges and needn't reach their ends.
Inputs may be any that keep to these rules, and one draw needn't show every extreme that they name: `tile_source`: entries 0 to 7 name the subdomain's own blocks, 8 + j the j-th block received from the previous subdomain and 10 + j the j-th from the next; subdomains form a closed loop. Slot 0 of each block is the block itself. Only the first tile_count[b] slots of destination block b are live; the others are not part of the graph. `send_blocks`: the 2 blocks of one list are distinct.
All inputs are finite; a program needn't handle non-finite values.
Results may differ from the reference program's by a relative error of at most 0.025.
Values may be sent and summed in bfloat16 or wider, within the bound.
A program may use at most 64 MiB of HBM per device.

```python
import math
import jax
import jax.numpy as jnp
from jax import lax

D = 128
BLOCK = 128
NB = 8
K = 4
SEND = 2
MB = 4
LAYERS = 4
BLOCKS = 64
NODES = 8192
N_DOM = 8


def draw_tile_source(key, part):
    spread = jax.random.randint(key, (BLOCKS, K), 0, NB + 2 * SEND)
    local_block = jnp.arange(BLOCKS, dtype=jnp.int32) % NB
    self_slot = local_block
    rim_slot = NB + local_block % (2 * SEND)
    slot_index = jnp.arange(K)[None, :]
    chosen = jnp.where(slot_index == 0, self_slot[:, None], jnp.where(slot_index == 1, rim_slot[:, None], spread))
    return chosen.astype(jnp.int32)


def draw_tile_count(key, part):
    domains = BLOCKS // NB
    subkeys = jax.random.split(key, 4)
    ceiling = jax.random.randint(subkeys[0], (domains,), 2, K + 1)
    hottest = jax.random.randint(subkeys[1], (), 0, domains)
    ceiling = jnp.where(jnp.arange(domains) == hottest, K, ceiling)
    drawn = jax.random.randint(subkeys[2], (domains, NB), 0, 1 << 20)
    counts = 2 + drawn % (ceiling[:, None] - 1)
    position = jax.random.randint(subkeys[3], (domains,), 0, NB)
    counts = jnp.where(jnp.arange(NB)[None, :] == position[:, None], ceiling[:, None], counts)
    return counts.reshape(BLOCKS).astype(jnp.int32)


def draw_send_blocks(key, part):
    domains = BLOCKS // NB
    scores = jax.random.randint(key, (domains, 2, NB), 0, 1 << 16) * NB + jnp.arange(NB)
    ranking = jnp.argsort(scores, axis=-1, stable=True)
    return ranking[:, :, :SEND].astype(jnp.int32)


def block_levels(key, dims, cuts, low, top_value):
    loudness = 1.0
    for axis_at, blocks in cuts:
        draws = jax.random.uniform(jax.random.fold_in(jax.random.fold_in(key, 6), axis_at), (blocks,), jnp.float32, low / len(cuts), top_value / len(cuts))
        loudness = loudness * jnp.repeat(jnp.exp(draws), dims[axis_at] // blocks).reshape((-1,) + (1,) * (len(dims) - 1 - axis_at))
    return loudness


def gaussian(rng, shape, scale, bound, cuts=(), held_as=jnp.bfloat16):
    loudness = block_levels(rng, shape, cuts, -0.22, 0.18) if cuts else 1.0
    result = jax.random.normal(rng, shape, jnp.float32) * scale * loudness
    return jnp.minimum(jnp.maximum(result, -bound), bound).astype(held_as)


def setup_inputs(seed: int = 0) -> dict:
    keys = jax.random.split(jax.random.key(seed), 12)
    node_latents = gaussian(keys[0], (LAYERS, MB, NODES, D), 1.0, 6.0, ((0, 4), (2, 8)))
    cotangent = gaussian(keys[1], (MB, NODES, D), 1.0, 6.0, ((1, 8),))
    tile_weights = gaussian(keys[2], (BLOCKS, K, BLOCK, BLOCK), (BLOCK * K) ** -0.5, 0.25, ((0, 8),))
    tile_source = draw_tile_source(jax.random.fold_in(keys[11], 71), 0)
    tile_count = draw_tile_count(jax.random.fold_in(keys[11], 71), 0)
    send_blocks = draw_send_blocks(jax.random.fold_in(keys[11], 71), 0)
    w_message = gaussian(keys[6], (LAYERS, D, D), D ** -0.5, 0.5, ((0, 4),))
    w_first = gaussian(keys[7], (LAYERS, 2 * D, D), (2 * D) ** -0.5, 0.375, ((0, 4),))
    bias_first = gaussian(keys[8], (LAYERS, D), 0.5, 3.0, ((0, 4),), jnp.float32)
    w_second = gaussian(keys[9], (LAYERS, D, D), D ** -0.5, 0.5, ((0, 4),))
    norm_gain = jnp.clip(1.0 + 0.18 * jax.random.normal(keys[10], (LAYERS, D), jnp.float32), 0.1, 1.9)
    return {"node_latents": node_latents, "cotangent": cotangent, "tile_weights": tile_weights, "tile_source": tile_source, "tile_count": tile_count, "send_blocks": send_blocks, "w_message": w_message, "w_first": w_first, "bias_first": bias_first, "w_second": w_second, "norm_gain": norm_gain}


epsilon = 1e-05

def device_pass(latent_rows, extended, tile_blocks, sources, counts, cotangent_rows, weight_first, bias_vector, weight_second, gain_vector):
    block_total, slot_total = sources.shape
    block_size = tile_blocks.shape[-1]
    feature_width = latent_rows.shape[-1]
    gathered = extended[sources].astype(jnp.float32)
    live_slots = jnp.arange(slot_total)[None, :] < counts[:, None]
    coupling = jnp.where(live_slots[:, :, None, None], tile_blocks, jnp.zeros_like(tile_blocks)).astype(jnp.float32)
    aggregate = jnp.einsum('bkij,bkjf->bif', coupling, gathered)
    aggregate = aggregate.reshape(block_total * block_size, feature_width).astype(jnp.bfloat16)
    joined = jnp.concatenate([latent_rows, aggregate], axis=1)
    before = jnp.dot(joined, weight_first, preferred_element_type=jnp.float32) + bias_vector
    hidden = jax.nn.silu(before).astype(jnp.bfloat16)
    output = jnp.dot(hidden, weight_second, preferred_element_type=jnp.float32)
    centred = output - lax.optimization_barrier(jnp.mean(output, axis=-1, keepdims=True))
    inverse = lax.rsqrt(lax.optimization_barrier(jnp.mean(centred * centred, axis=-1, keepdims=True)) + epsilon)
    normed = centred * inverse
    incoming = cotangent_rows.astype(jnp.float32)
    grad_gain = lax.optimization_barrier(jnp.sum(incoming * normed, axis=0))
    scaled = incoming * gain_vector
    grad_out = inverse * (scaled - lax.optimization_barrier(jnp.mean(scaled, axis=-1, keepdims=True)) - normed * lax.optimization_barrier(jnp.mean(scaled * normed, axis=-1, keepdims=True)))
    grad_out = grad_out.astype(jnp.bfloat16)
    grad_second = jnp.dot(hidden.T, grad_out, preferred_element_type=jnp.float32)
    grad_hidden = jnp.dot(grad_out, weight_second.T, preferred_element_type=jnp.float32)
    sigmoid = jax.nn.sigmoid(before)
    grad_before = (grad_hidden * sigmoid * (1.0 + before * (1.0 - sigmoid))).astype(jnp.bfloat16)
    grad_bias = lax.optimization_barrier(jnp.sum(grad_before.astype(jnp.float32), axis=0))
    grad_first = jnp.dot(joined.T, grad_before, preferred_element_type=jnp.float32)
    grad_joined = jnp.dot(grad_before, weight_first.T, preferred_element_type=jnp.float32)
    grad_aggregate = grad_joined[:, feature_width:].astype(jnp.bfloat16).reshape(block_total, block_size, feature_width)
    grad_gathered = jnp.einsum('bkij,bif->bkjf', coupling, grad_aggregate.astype(jnp.float32))
    grad_extended = jax.ops.segment_sum(grad_gathered.reshape(block_total * slot_total, block_size, feature_width), sources.reshape(-1), num_segments=extended.shape[0])
    return (grad_joined[:, :feature_width], grad_extended, grad_first, grad_bias, grad_second, grad_gain)

def take_rows(values, indices):
    return values[indices]

def add_rows(target, indices, addend):
    return target.at[indices].add(addend)

def micro_pass(latents, cotangent_rows, tile_blocks, sources, counts, send_blocks, weight_message, weight_first, bias_vector, weight_second, gain_vector):
    feature_width = latents.shape[-1]
    node_total = latents.shape[0]
    messages = jnp.dot(latents, weight_message, preferred_element_type=jnp.float32).astype(jnp.bfloat16)
    messages = messages.reshape(N_DOM, NB, BLOCK, feature_width)
    sent_left = jax.vmap(take_rows)(messages, send_blocks[:, 0])
    sent_right = jax.vmap(take_rows)(messages, send_blocks[:, 1])
    extended = jnp.concatenate([messages, jnp.roll(sent_right, 1, axis=0), jnp.roll(sent_left, -1, axis=0)], axis=1)

    def one_device(pieces):
        return device_pass(pieces[0], pieces[1], pieces[2], pieces[3], pieces[4], pieces[5], weight_first, bias_vector, weight_second, gain_vector)
    partial_joined, grad_extended, grad_first, grad_bias, grad_second, grad_gain = lax.map(one_device, (latents.reshape(N_DOM, NB * BLOCK, feature_width), extended, tile_blocks, sources, counts, cotangent_rows.reshape(N_DOM, NB * BLOCK, feature_width)))
    back_right = jnp.roll(grad_extended[:, NB:NB + SEND], -1, axis=0)
    back_left = jnp.roll(grad_extended[:, NB + SEND:], 1, axis=0)
    grad_messages = jax.vmap(add_rows)(grad_extended[:, :NB], send_blocks[:, 1], back_right)
    grad_messages = jax.vmap(add_rows)(grad_messages, send_blocks[:, 0], back_left)
    grad_messages = grad_messages.astype(jnp.bfloat16).reshape(node_total, feature_width)
    grad_message = jnp.dot(latents.T, grad_messages, preferred_element_type=jnp.float32)
    grad_latents = cotangent_rows.astype(jnp.float32) + partial_joined.reshape(node_total, feature_width)
    grad_latents = (grad_latents + jnp.dot(grad_messages, weight_message.T, preferred_element_type=jnp.float32)).astype(jnp.bfloat16)
    return (grad_latents, (grad_message, lax.optimization_barrier(jnp.sum(grad_first, axis=0)), lax.optimization_barrier(jnp.sum(grad_bias, axis=0)), lax.optimization_barrier(jnp.sum(grad_second, axis=0)), lax.optimization_barrier(jnp.sum(grad_gain, axis=0))))

def reference(node_latents, cotangent, tile_weights, tile_source, tile_count, send_blocks, w_message, w_first, bias_first, w_second, norm_gain):
    tile_blocks = tile_weights.reshape(N_DOM, NB, K, BLOCK, BLOCK)
    sources = tile_source.reshape(N_DOM, NB, K)
    counts = tile_count.reshape(N_DOM, NB)
    incoming = cotangent
    stored = [None] * LAYERS
    weight_grads = [None] * LAYERS
    for layer_index in range(LAYERS - 1, -1, -1):

        def one_micro(pieces):
            return micro_pass(pieces[0], pieces[1], tile_blocks, sources, counts, send_blocks, w_message[layer_index], w_first[layer_index], bias_first[layer_index], w_second[layer_index], norm_gain[layer_index])
        incoming, sums = lax.map(one_micro, (node_latents[layer_index], incoming))
        stored[layer_index] = incoming
        weight_grads[layer_index] = tuple((lax.optimization_barrier(jnp.sum(entry, axis=0)) for entry in sums))
    normaliser = 1.0 / math.sqrt(MB * NODES)
    return (jnp.stack(stored), jnp.stack([entry[0] for entry in weight_grads]) * normaliser, jnp.stack([entry[1] for entry in weight_grads]) * normaliser, jnp.stack([entry[2] for entry in weight_grads]) * normaliser, jnp.stack([entry[3] for entry in weight_grads]) * normaliser, jnp.stack([entry[4] for entry in weight_grads]) * normaliser)
```

```python
import functools
import math

import jax
import jax.numpy as jnp
from jax import lax
from jax.experimental import pallas as pl
from jax.experimental.pallas import tpu as pltpu
from jax.sharding import PartitionSpec as P

epsilon = 1e-05
MESH = pl.DeviceIdType.MESH
F32 = jnp.float32
BF16 = jnp.bfloat16


def mm(a, b):
    return jnp.dot(a, b, preferred_element_type=F32)


def mm_nt(a, b):
    return lax.dot_general(a, b, (((1,), (1,)), ((), ())), preferred_element_type=F32)


def mm_tn(a, b):
    return lax.dot_general(a, b, (((0,), (0,)), ((), ())), preferred_element_type=F32)


def kernel(
    n,
    sections,
    chunk,
    normaliser,
    source_ref,
    count_ref,
    send_ref,
    latents_ref,
    cotangent_ref,
    tiles_ref,
    w_message_ref,
    w_first_ref,
    bias_ref,
    w_second_ref,
    gain_ref,
    out_ref,
    out_message_ref,
    out_first_ref,
    out_bias_ref,
    out_second_ref,
    out_gain_ref,
    incoming,
    messages,
    extended,
    outbox,
    dense,
    dense_t,
    aggregates,
    hiddens,
    normeds,
    inverses,
    factors,
    partial,
    grad_own,
    backbox,
    backs,
    totals,
    red_send,
    red_recv,
    gathered,
    cot_sem,
    out_send,
    out_recv,
    back_send,
    back_recv,
    sec_send,
    sec_recv,
    rs_send,
    rs_recv,
    ag_send,
    ag_recv,
):
    me = lax.axis_index("dom")
    section = lax.axis_index("section")
    is_last = section == sections - 1
    right, left = lax.rem(me + 1, n), lax.rem(me + n - 1, n)
    micros, rows, width = latents_ref.shape
    blocks, slots, size, _ = tiles_ref.shape
    entries = extended.shape[1]
    sends = (entries - blocks) // 2

    barrier = pltpu.get_barrier_semaphore()

    def greet(offset, carry):
        pl.semaphore_signal(
            barrier, inc=1, device_id=(lax.rem(me + offset, n), section), device_id_type=MESH
        )
        return carry

    lax.fori_loop(1, n, greet, 0)

    @pl.when(section > 0)
    def _():
        pl.semaphore_signal(barrier, inc=1, device_id=(me, section - 1), device_id_type=MESH)

    @pl.when(jnp.logical_not(is_last))
    def _():
        pl.semaphore_signal(barrier, inc=1, device_id=(me, section + 1), device_id_type=MESH)

    cot_copy = pltpu.make_async_copy(cotangent_ref, incoming, cot_sem)

    @pl.when(is_last)
    def _():
        cot_copy.start()

    def make_messages(m, carry):
        value = mm(latents_ref[m], w_message_ref[...]).astype(BF16)
        value = value.reshape(blocks, size, width)
        extended[m, 0:blocks] = value
        messages[...] = value
        for side in range(2):
            for j in range(sends):
                outbox[m, side, j] = messages[send_ref[side * sends + j]]
        return carry

    lax.fori_loop(0, micros, make_messages, 0)
    pl.semaphore_wait(
        barrier, n - 1 + jnp.where(section > 0, 1, 0) + jnp.where(is_last, 0, 1)
    )

    def halo_copy(m, side):
        start = blocks + (0 if side == 1 else sends)
        return pltpu.make_async_remote_copy(
            src_ref=outbox.at[m, side],
            dst_ref=extended.at[m, pl.ds(start, sends)],
            send_sem=out_send.at[m, side],
            recv_sem=out_recv.at[m, side],
            device_id=(right if side == 1 else left, section),
            device_id_type=MESH,
        )

    def back_copy(m, side):
        return pltpu.make_async_remote_copy(
            src_ref=backbox.at[m, side],
            dst_ref=backs.at[m, side],
            send_sem=back_send.at[m, side],
            recv_sem=back_recv.at[m, side],
            device_id=(left if side == 0 else right, section),
            device_id_type=MESH,
        )

    def section_copy(m):
        return pltpu.make_async_remote_copy(
            src_ref=out_ref.at[m],
            dst_ref=incoming.at[m],
            send_sem=sec_send.at[m],
            recv_sem=sec_recv.at[m],
            device_id=(me, section - 1),
            device_id_type=MESH,
        )

    def start_halo(m, carry):
        halo_copy(m, 0).start()
        halo_copy(m, 1).start()
        return carry

    lax.fori_loop(0, micros, start_halo, 0)

    def build(b, carry):
        live = [k < count_ref[b] for k in range(slots)]
        tiles = [tiles_ref[b, k].astype(F32) for k in range(slots)]
        flipped = [tile.T for tile in tiles]
        column = pl.ds(pl.multiple_of(b * size, size), size)
        for e in range(entries):
            value = jnp.zeros((size, size), F32)
            value_t = jnp.zeros((size, size), F32)
            for k in range(slots):
                hit = jnp.logical_and(source_ref[b * slots + k] == e, live[k])
                weight = jnp.where(hit, 1.0, 0.0).astype(F32)
                value = value + tiles[k] * weight
                value_t = value_t + flipped[k] * weight
            dense[b, :, e * size : (e + 1) * size] = value.astype(BF16)
            dense_t[e * size : (e + 1) * size, column] = value_t.astype(BF16)
        return carry

    lax.fori_loop(0, blocks, build, 0)

    totals[...] = jnp.zeros_like(totals)

    def forward(m):
        halo_copy(m, 0).wait()
        halo_copy(m, 1).wait()
        coupling = dense[...].reshape(rows, entries * size)
        aggregate = mm(coupling, extended[m].reshape(entries * size, width)).astype(BF16)
        aggregates[m] = aggregate
        joined = jnp.concatenate([latents_ref[m], aggregate], axis=1)
        before = mm(joined, w_first_ref[...]) + bias_ref[...]
        sigmoid = 1.0 / (1.0 + jnp.exp(-before))
        hidden = (before * sigmoid).astype(BF16)
        hiddens[m] = hidden
        factors[m] = sigmoid * (1.0 + before * (1.0 - sigmoid))
        output = mm(hidden, w_second_ref[...])
        centred = output - jnp.mean(output, axis=-1, keepdims=True)
        inverse = lax.rsqrt(jnp.mean(centred * centred, axis=-1, keepdims=True) + epsilon)
        normeds[m] = centred * inverse
        inverses[m] = inverse

    def upfront(m, carry):
        forward(m)
        return carry

    lax.fori_loop(0, jnp.where(is_last, 1, micros), upfront, 0)

    @pl.when(is_last)
    def _():
        cot_copy.wait()

    def turn(m, carry):
        @pl.when(jnp.logical_not(is_last))
        def _():
            section_copy(m).wait_recv()

        value = incoming[m].astype(F32)
        normed = normeds[m]
        gain_row = jnp.sum(value * normed, axis=0, keepdims=True)
        scaled = value * gain_ref[...]
        grad_out = inverses[m] * (
            scaled
            - jnp.mean(scaled, axis=-1, keepdims=True)
            - normed * jnp.mean(scaled * normed, axis=-1, keepdims=True)
        )
        grad_out = grad_out.astype(BF16)
        grad_before = (mm_nt(grad_out, w_second_ref[...]) * factors[m]).astype(BF16)
        grad_joined = mm_nt(grad_before, w_first_ref[...])
        partial[...] = value + grad_joined[:, :width]
        grad_aggregate = grad_joined[:, width:].astype(BF16)
        rim = mm(dense_t[blocks * size :, :], grad_aggregate).astype(BF16)
        backbox[m] = rim.reshape(2, sends, size, width)
        back_copy(m, 0).start()
        back_copy(m, 1).start()
        own = mm(dense_t[: blocks * size, :], grad_aggregate)
        grad_own[...] = own.reshape(blocks, size, width)
        joined = jnp.concatenate([latents_ref[m], aggregates[m]], axis=1)
        totals[width : 3 * width] += mm_tn(joined, grad_before)
        totals[3 * width : 4 * width] += mm_tn(hiddens[m], grad_out)
        bias_row = jnp.sum(grad_before.astype(F32), axis=0, keepdims=True)
        totals[4 * width : 4 * width + 1] += bias_row
        totals[4 * width + 1 : 4 * width + 2] += gain_row

        ahead = jnp.where(is_last, jnp.minimum(m + 2, micros), m + 1)
        lax.fori_loop(m + 1, ahead, upfront, 0)

        back_copy(m, 0).wait()
        back_copy(m, 1).wait()
        pieces = []
        for i in range(blocks):
            piece = grad_own[i]
            for j in range(sends):
                to_next = jnp.where(send_ref[sends + j] == i, 1.0, 0.0).astype(F32)
                to_previous = jnp.where(send_ref[j] == i, 1.0, 0.0).astype(F32)
                piece = piece + backs[m, 0, j].astype(F32) * to_next
                piece = piece + backs[m, 1, j].astype(F32) * to_previous
            pieces.append(piece.astype(BF16))
        grad_messages = jnp.concatenate(pieces, axis=0)
        result = partial[...] + mm_nt(grad_messages, w_message_ref[...])
        out_ref[m] = result.astype(BF16)

        @pl.when(section > 0)
        def _():
            section_copy(m).start()

        totals[0:width] += mm_tn(latents_ref[m], grad_messages)
        return carry

    lax.fori_loop(0, micros, turn, 0)

    red_send[...] = totals[...].astype(BF16)

    def part(index):
        return pl.ds(pl.multiple_of(index * chunk, 16), chunk)

    def rs_copy(offset):
        peer = lax.rem(me + offset, n)
        return pltpu.make_async_remote_copy(
            src_ref=red_send.at[part(peer)],
            dst_ref=red_recv.at[offset - 1],
            send_sem=rs_send.at[offset - 1],
            recv_sem=rs_recv.at[offset - 1],
            device_id=(peer, section),
            device_id_type=MESH,
        )

    def ag_copy(offset):
        return pltpu.make_async_remote_copy(
            src_ref=gathered.at[part(me)],
            dst_ref=gathered.at[part(me)],
            send_sem=ag_send.at[offset - 1],
            recv_sem=ag_recv.at[offset - 1],
            device_id=(lax.rem(me + offset, n), section),
            device_id_type=MESH,
        )

    def ag_arrival(offset):
        owner = lax.rem(me + n - offset, n)
        return pltpu.make_async_remote_copy(
            src_ref=gathered.at[part(owner)],
            dst_ref=gathered.at[part(owner)],
            send_sem=ag_send.at[offset - 1],
            recv_sem=ag_recv.at[offset - 1],
            device_id=(lax.rem(me + offset, n), section),
            device_id_type=MESH,
        )

    def each(body):
        def step(offset, carry):
            body(offset)
            return carry

        lax.fori_loop(1, n, step, 0)

    each(lambda offset: rs_copy(offset).start())

    def collect(offset, total):
        rs_copy(offset).wait()
        return total + red_recv[offset - 1].astype(F32)

    total = lax.fori_loop(1, n, collect, totals[part(me), :])
    gathered[part(me), :] = (total * normaliser).astype(BF16)
    each(lambda offset: ag_copy(offset).start())

    def finish_section(m, carry):
        section_copy(m).wait_send()
        return carry

    @pl.when(section > 0)
    def _():
        lax.fori_loop(0, micros, finish_section, 0)

    each(lambda offset: ag_arrival(offset).wait_recv())
    each(lambda offset: ag_copy(offset).wait_send())
    out_message_ref[...] = gathered[0:width].astype(F32)
    out_first_ref[...] = gathered[width : 3 * width].astype(F32)
    out_second_ref[...] = gathered[3 * width : 4 * width].astype(F32)
    tail = gathered[4 * width : 4 * width + 16].astype(F32)
    out_bias_ref[...] = tail[0:1]
    out_gain_ref[...] = tail[1:2]


def per_device(
    n,
    sections,
    node_latents,
    cotangent,
    tile_weights,
    tile_source,
    tile_count,
    send_blocks,
    w_message,
    w_first,
    bias_first,
    w_second,
    norm_gain,
):
    micros, rows, width = cotangent.shape
    blocks, slots, size, _ = tile_weights.shape
    sends = send_blocks.shape[2]
    entries = blocks + 2 * sends
    total_rows = 4 * width + 16
    chunk = -(-total_rows // (16 * n)) * 16
    normaliser = 1.0 / math.sqrt(micros * rows * n)
    vmem = pl.BlockSpec(memory_space=pltpu.VMEM)
    smem = pl.BlockSpec(memory_space=pltpu.SMEM)
    dma = pltpu.SemaphoreType.DMA
    results = pl.pallas_call(
        functools.partial(kernel, n, sections, chunk, normaliser),
        out_shape=(
            jax.ShapeDtypeStruct((micros, rows, width), BF16),
            jax.ShapeDtypeStruct((width, width), F32),
            jax.ShapeDtypeStruct((2 * width, width), F32),
            jax.ShapeDtypeStruct((1, width), F32),
            jax.ShapeDtypeStruct((width, width), F32),
            jax.ShapeDtypeStruct((1, width), F32),
        ),
        in_specs=[smem] * 3 + [vmem, pl.BlockSpec(memory_space=pl.ANY)] + [vmem] * 6,
        out_specs=(vmem,) * 6,
        scratch_shapes=[
            pltpu.VMEM((micros, rows, width), BF16),
            pltpu.VMEM((blocks, size, width), BF16),
            pltpu.VMEM((micros, entries, size, width), BF16),
            pltpu.VMEM((micros, 2, sends, size, width), BF16),
            pltpu.VMEM((blocks, size, entries * size), BF16),
            pltpu.VMEM((entries * size, blocks * size), BF16),
            pltpu.VMEM((micros, rows, width), BF16),
            pltpu.VMEM((micros, rows, width), BF16),
            pltpu.VMEM((micros, rows, width), F32),
            pltpu.VMEM((micros, rows, 1), F32),
            pltpu.VMEM((micros, rows, width), F32),
            pltpu.VMEM((rows, width), F32),
            pltpu.VMEM((blocks, size, width), F32),
            pltpu.VMEM((micros, 2, sends, size, width), BF16),
            pltpu.VMEM((micros, 2, sends, size, width), BF16),
            pltpu.VMEM((n * chunk, width), F32),
            pltpu.VMEM((n * chunk, width), BF16),
            pltpu.VMEM((n - 1, chunk, width), BF16),
            pltpu.VMEM((n * chunk, width), BF16),
            dma(()),
            dma((micros, 2)),
            dma((micros, 2)),
            dma((micros, 2)),
            dma((micros, 2)),
            dma((micros,)),
            dma((micros,)),
            dma((n - 1,)),
            dma((n - 1,)),
            dma((n - 1,)),
            dma((n - 1,)),
        ],
        compiler_params=pltpu.CompilerParams(
            collective_id=0, has_side_effects=True, vmem_limit_bytes=56 * 1024 * 1024
        ),
    )(
        tile_source.reshape(-1),
        tile_count,
        send_blocks.reshape(-1),
        node_latents[0],
        cotangent,
        tile_weights,
        w_message[0],
        w_first[0],
        bias_first,
        w_second[0],
        norm_gain,
    )
    grads, message, first, bias, second, gain = results
    return (grads[None], message[None], first[None], bias, second[None], gain)


def solution(mesh):
    return jax.shard_map(
        functools.partial(per_device, mesh.shape["dom"], mesh.shape["section"]),
        mesh=mesh,
        in_specs=(
            P("section", None, "dom", None),
            P(None, "dom", None),
            P("dom", None, None, None),
            P("dom", None),
            P("dom"),
            P("dom", None, None),
            P("section", None, None),
            P("section", None, None),
            P("section", None),
            P("section", None, None),
            P("section", None),
        ),
        out_specs=(
            P("section", None, "dom", None),
            P("section", None, None),
            P("section", None, None),
            P("section", None),
            P("section", None, None),
            P("section", None),
        ),
        check_vma=False,
    )
```

```python
import functools
import math

import jax
import jax.numpy as jnp
from jax import lax
from jax.experimental import pallas as pl
from jax.experimental.pallas import tpu as pltpu
from jax.sharding import PartitionSpec as P

epsilon = 1e-05
MESH = pl.DeviceIdType.MESH
F32 = jnp.float32
BF16 = jnp.bfloat16
parts = 2


def mm(a, b):
    return jnp.dot(a, b, preferred_element_type=F32)


def mm_nt(a, b):
    return lax.dot_general(a, b, (((1,), (1,)), ((), ())), preferred_element_type=F32)


def mm_tn(a, b):
    return lax.dot_general(a, b, (((0,), (0,)), ((), ())), preferred_element_type=F32)


def kernel(
    n,
    sections,
    chunks,
    normaliser,
    source_ref,
    count_ref,
    send_ref,
    latents_hbm,
    cotangent_ref,
    tiles_hbm,
    w_message_hbm,
    w_first_hbm,
    bias_hbm,
    w_second_hbm,
    gain_hbm,
    out_ref,
    gathered_a,
    gathered_b,
    w_message_ref,
    w_first_ref,
    bias_ref,
    w_second_ref,
    gain_ref,
    weight_sem,
    latents_ref,
    tiles_ref,
    incoming,
    messages,
    extended,
    outbox,
    dense,
    dense_t,
    aggregates,
    hiddens,
    normeds,
    inverses,
    factors,
    partial,
    grad_own,
    grad_outs,
    grad_befores,
    grad_aggregates,
    backbox,
    backs,
    totals,
    message_total,
    send_a,
    recv_a,
    send_b,
    recv_b,
    cot_sem,
    latents_sem,
    tiles_sem,
    out_send,
    out_recv,
    back_send,
    back_recv,
    sec_send,
    sec_recv,
    rs_send_a,
    rs_recv_a,
    ag_send_a,
    ag_recv_a,
    rs_send_b,
    rs_recv_b,
    ag_send_b,
    ag_recv_b,
):
    me = lax.axis_index("dom")
    section = lax.axis_index("section")
    is_last = section == sections - 1
    right, left = lax.rem(me + 1, n), lax.rem(me + n - 1, n)
    micros, rows, width = latents_ref.shape
    blocks, slots, size, _ = tiles_ref.shape
    entries = extended.shape[1]
    sends = (entries - blocks) // 2

    barrier = pltpu.get_barrier_semaphore()

    def greet(offset, carry):
        pl.semaphore_signal(
            barrier, inc=1, device_id=(lax.rem(me + offset, n), section), device_id_type=MESH
        )
        return carry

    lax.fori_loop(1, n, greet, 0)

    @pl.when(section > 0)
    def _():
        pl.semaphore_signal(barrier, inc=1, device_id=(me, section - 1), device_id_type=MESH)

    @pl.when(jnp.logical_not(is_last))
    def _():
        pl.semaphore_signal(barrier, inc=1, device_id=(me, section + 1), device_id_type=MESH)

    def latents_copy(m):
        return pltpu.make_async_copy(latents_hbm.at[m], latents_ref.at[m], latents_sem.at[m])

    message_copy = pltpu.make_async_copy(w_message_hbm, w_message_ref, weight_sem.at[0])
    weight_copies = [
        pltpu.make_async_copy(w_first_hbm, w_first_ref, weight_sem.at[1]),
        pltpu.make_async_copy(bias_hbm, bias_ref, weight_sem.at[2]),
        pltpu.make_async_copy(w_second_hbm, w_second_ref, weight_sem.at[3]),
        pltpu.make_async_copy(gain_hbm, gain_ref, weight_sem.at[4]),
    ]
    message_copy.start()
    for m in range(micros):
        latents_copy(m).start()
    for copy in weight_copies:
        copy.start()
    tiles_copy = pltpu.make_async_copy(tiles_hbm, tiles_ref, tiles_sem)
    tiles_copy.start()

    cot_copy = pltpu.make_async_copy(cotangent_ref, incoming, cot_sem)

    @pl.when(is_last)
    def _():
        cot_copy.start()

    def make_messages(m, carry):
        latents_copy(m).wait()
        value = mm(latents_ref[m], w_message_ref[...]).astype(BF16)
        value = value.reshape(blocks, size, width)
        extended[m, 0:blocks] = value
        messages[...] = value
        for side in range(2):
            for j in range(sends):
                outbox[m, side, j] = messages[send_ref[side, j]]
        return carry

    message_copy.wait()
    make_messages(0, 0)
    pl.semaphore_wait(
        barrier, n - 1 + jnp.where(section > 0, 1, 0) + jnp.where(is_last, 0, 1)
    )

    def halo_copy(m, side):
        start = blocks + (0 if side == 1 else sends)
        return pltpu.make_async_remote_copy(
            src_ref=outbox.at[m, side],
            dst_ref=extended.at[m, pl.ds(start, sends)],
            send_sem=out_send.at[m, side],
            recv_sem=out_recv.at[m, side],
            device_id=(right if side == 1 else left, section),
            device_id_type=MESH,
        )

    def back_copy(m, side):
        return pltpu.make_async_remote_copy(
            src_ref=backbox.at[m, side],
            dst_ref=backs.at[m, side],
            send_sem=back_send.at[m, side],
            recv_sem=back_recv.at[m, side],
            device_id=(left if side == 0 else right, section),
            device_id_type=MESH,
        )

    part_rows = rows // parts

    def section_copy(m, q):
        span = pl.ds(q * part_rows, part_rows)
        return pltpu.make_async_remote_copy(
            src_ref=out_ref.at[m, span],
            dst_ref=incoming.at[m, span],
            send_sem=sec_send.at[m, q],
            recv_sem=sec_recv.at[m, q],
            device_id=(me, section - 1),
            device_id_type=MESH,
        )

    def start_halo(m, carry):
        halo_copy(m, 0).start()
        halo_copy(m, 1).start()
        return carry

    start_halo(0, 0)
    lax.fori_loop(1, micros, make_messages, 0)
    start_halo(1, 0)
    for copy in weight_copies:
        copy.wait()
    tiles_copy.wait()

    def build(b, carry):
        live = [k < count_ref[b] for k in range(slots)]
        tiles = [tiles_ref[b, k].astype(F32) for k in range(slots)]
        flipped = [tile.T for tile in tiles]
        column = pl.ds(pl.multiple_of(b * size, size), size)
        for e in range(entries):
            value = jnp.zeros((size, size), F32)
            value_t = jnp.zeros((size, size), F32)
            for k in range(slots):
                hit = jnp.logical_and(source_ref[k, b] == e, live[k])
                weight = jnp.where(hit, 1.0, 0.0).astype(F32)
                value = value + tiles[k] * weight
                value_t = value_t + flipped[k] * weight
            dense[b, :, e * size : (e + 1) * size] = value.astype(BF16)
            dense_t[e * size : (e + 1) * size, column] = value_t.astype(BF16)
        return carry

    lax.fori_loop(0, blocks, build, 0)

    totals[...] = jnp.zeros_like(totals)
    message_total[...] = jnp.zeros_like(message_total)

    def forward(m):
        halo_copy(m, 0).wait_recv()
        halo_copy(m, 1).wait_recv()
        lax.fori_loop(jnp.minimum(m + 2, micros), jnp.minimum(m + 3, micros), start_halo, 0)
        coupling = dense[...].reshape(rows, entries * size)
        aggregate = mm(coupling, extended[m].reshape(entries * size, width)).astype(BF16)
        aggregates[m] = aggregate
        joined = jnp.concatenate([latents_ref[m], aggregate], axis=1)
        before = mm(joined, w_first_ref[...]) + bias_ref[...]
        sigmoid = 1.0 / (1.0 + jnp.exp(-before))
        hidden = (before * sigmoid).astype(BF16)
        hiddens[m] = hidden
        factors[m] = sigmoid * (1.0 + before * (1.0 - sigmoid))
        output = mm(hidden, w_second_ref[...])
        centred = output - jnp.mean(output, axis=-1, keepdims=True)
        inverse = lax.rsqrt(jnp.mean(centred * centred, axis=-1, keepdims=True) + epsilon)
        normeds[m] = centred * inverse
        inverses[m] = inverse

    def upfront(m, carry):
        forward(m)
        return carry

    @pl.when(is_last)
    def _():
        cot_copy.wait()

    def row_part(index, chunk):
        return pl.ds(pl.multiple_of(index * chunk, 16), chunk)

    def reduction(chunk, source, landing, result, sems):
        rs_send, rs_recv, ag_send, ag_recv = sems

        def rs_copy(offset):
            peer = lax.rem(me + offset, n)
            return pltpu.make_async_remote_copy(
                src_ref=source.at[row_part(peer, chunk)],
                dst_ref=landing.at[offset - 1],
                send_sem=rs_send.at[offset - 1],
                recv_sem=rs_recv.at[offset - 1],
                device_id=(peer, section),
                device_id_type=MESH,
            )

        def ag_copy(offset, owner):
            return pltpu.make_async_remote_copy(
                src_ref=result.at[row_part(owner, chunk)],
                dst_ref=result.at[row_part(owner, chunk)],
                send_sem=ag_send.at[offset - 1],
                recv_sem=ag_recv.at[offset - 1],
                device_id=(lax.rem(me + offset, n), section),
                device_id_type=MESH,
            )

        def each(body):
            def step(offset, carry):
                body(offset)
                return carry

            lax.fori_loop(1, n, step, 0)

        def scatter(total):
            source[...] = total[...].astype(BF16)
            each(lambda offset: rs_copy(offset).start())

        def gather(total):
            def collect(offset, value):
                rs_copy(offset).wait()
                return value + landing[offset - 1].astype(F32)

            value = lax.fori_loop(1, n, collect, total[row_part(me, chunk), :])
            result[row_part(me, chunk), :] = (value * normaliser).astype(BF16)
            each(lambda offset: ag_copy(offset, me).start())

        def finish():
            each(lambda offset: ag_copy(offset, lax.rem(me + n - offset, n)).wait_recv())
            each(lambda offset: ag_copy(offset, me).wait_send())

        return scatter, gather, finish

    scatter_a, gather_a, finish_a = reduction(
        chunks[0], send_a, recv_a, gathered_a, (rs_send_a, rs_recv_a, ag_send_a, ag_recv_a)
    )
    scatter_b, gather_b, finish_b = reduction(
        chunks[1], send_b, recv_b, gathered_b, (rs_send_b, rs_recv_b, ag_send_b, ag_recv_b)
    )

    def first_half(m, carry):
        slot = lax.rem(m, 2)
        gain_row = jnp.zeros((1, width), F32)
        bias_row = jnp.zeros((1, width), F32)
        for q in range(parts):
            span = slice(q * part_rows, (q + 1) * part_rows)

            @pl.when(jnp.logical_not(is_last))
            def _():
                section_copy(m, q).wait_recv()

            value = incoming[m, span].astype(F32)
            normed = normeds[m, span]
            gain_row += jnp.sum(value * normed, axis=0, keepdims=True)
            scaled = value * gain_ref[...]
            grad_out = inverses[m, span] * (
                scaled
                - jnp.mean(scaled, axis=-1, keepdims=True)
                - normed * jnp.mean(scaled * normed, axis=-1, keepdims=True)
            )
            grad_out = grad_out.astype(BF16)
            grad_outs[span] = grad_out
            grad_before = (mm_nt(grad_out, w_second_ref[...]) * factors[m, span]).astype(BF16)
            grad_befores[span] = grad_before
            bias_row += jnp.sum(grad_before.astype(F32), axis=0, keepdims=True)
            grad_joined = mm_nt(grad_before, w_first_ref[...])
            partial[slot, span] = value + grad_joined[:, :width]
            grad_aggregates[span] = grad_joined[:, width:].astype(BF16)
        for side in range(2):
            start = (blocks + side * sends) * size
            rim = mm(dense_t[start : start + sends * size, :], grad_aggregates[...])
            backbox[m, side] = rim.astype(BF16).reshape(sends, size, width)
            back_copy(m, side).start()
        own = mm(dense_t[: blocks * size, :], grad_aggregates[...])
        grad_own[slot] = own.reshape(blocks, size, width)
        joined = jnp.concatenate([latents_ref[m], aggregates[m]], axis=1)
        totals[: 2 * width] += mm_tn(joined, grad_befores[...])
        totals[2 * width : 3 * width] += mm_tn(hiddens[m], grad_outs[...])
        totals[3 * width : 3 * width + 1] += bias_row
        totals[3 * width + 1 : 3 * width + 2] += gain_row

        return carry

    def second_half(m, carry):
        slot = lax.rem(m, 2)
        back_copy(m, 0).wait_recv()
        back_copy(m, 1).wait_recv()
        for q in range(parts):
            span = slice(q * part_rows, (q + 1) * part_rows)
            pieces = []
            for i in range(q * blocks // parts, (q + 1) * blocks // parts):
                piece = grad_own[slot, i]
                for j in range(sends):
                    to_next = jnp.where(send_ref[1, j] == i, 1.0, 0.0).astype(F32)
                    to_previous = jnp.where(send_ref[0, j] == i, 1.0, 0.0).astype(F32)
                    piece = piece + backs[m, 0, j].astype(F32) * to_next
                    piece = piece + backs[m, 1, j].astype(F32) * to_previous
                pieces.append(piece.astype(BF16))
            grad_messages = jnp.concatenate(pieces, axis=0)
            grad_outs[span] = grad_messages
            result = partial[slot, span] + mm_nt(grad_messages, w_message_ref[...])
            out_ref[m, span] = result.astype(BF16)

            @pl.when(section > 0)
            def _():
                section_copy(m, q).start()

        message_total[0:width] += mm_tn(latents_ref[m], grad_outs[...])
        return carry

    def turn(t, carry):
        start = jnp.where(is_last, t, jnp.where(t == 0, 0, micros))
        stop = jnp.where(is_last, jnp.minimum(t + 1, micros), micros)
        lax.fori_loop(start, stop, upfront, 0)
        lax.fori_loop(t, jnp.minimum(t + 1, micros), first_half, 0)

        @pl.when(t == micros)
        def _():
            scatter_a(totals)

        lax.fori_loop(jnp.maximum(t - 1, 0), t, second_half, 0)
        return carry

    lax.fori_loop(0, micros + 1, turn, 0)
    scatter_b(message_total)
    gather_a(totals)
    gather_b(message_total)

    def finish_halos(m, carry):
        for side in range(2):
            halo_copy(m, side).wait_send()
            back_copy(m, side).wait_send()
        return carry

    lax.fori_loop(0, micros, finish_halos, 0)

    def finish_section(m, carry):
        for q in range(parts):
            section_copy(m, q).wait_send()
        return carry

    @pl.when(section > 0)
    def _():
        lax.fori_loop(0, micros, finish_section, 0)

    finish_a()
    finish_b()


def unpack(grads_ref, a_ref, b_ref, out_ref, message_ref, first_ref, bias_ref, second_ref, gain_ref, sem):
    width = message_ref.shape[-1]
    copy = pltpu.make_async_copy(grads_ref, out_ref, sem)
    copy.start()
    message_ref[...] = b_ref[0:width].astype(F32)
    first_ref[...] = a_ref[0 : 2 * width].astype(F32)
    second_ref[...] = a_ref[2 * width : 3 * width].astype(F32)
    tail = a_ref[3 * width : 3 * width + 16].astype(F32)
    bias_ref[...] = tail[0:1]
    gain_ref[...] = tail[1:2]
    copy.wait()


def per_device(
    n,
    sections,
    node_latents,
    cotangent,
    tile_weights,
    tile_source,
    tile_count,
    send_blocks,
    w_message,
    w_first,
    bias_first,
    w_second,
    norm_gain,
):
    micros, rows, width = cotangent.shape
    blocks, slots, size, _ = tile_weights.shape
    sends = send_blocks.shape[2]
    entries = blocks + 2 * sends
    chunk_a = -(-(3 * width + 16) // (16 * n)) * 16
    chunk_b = -(-width // (16 * n)) * 16
    normaliser = 1.0 / math.sqrt(micros * rows * n)
    vmem = pl.BlockSpec(memory_space=pltpu.VMEM)
    smem = pl.BlockSpec(memory_space=pltpu.SMEM)
    anywhere = pl.BlockSpec(memory_space=pl.ANY)
    hbm = pl.BlockSpec(memory_space=pltpu.HBM)
    dma = pltpu.SemaphoreType.DMA
    grads, packed_a, packed_b = pl.pallas_call(
        functools.partial(kernel, n, sections, (chunk_a, chunk_b), normaliser),
        out_shape=(
            jax.ShapeDtypeStruct((micros, rows, width), BF16),
            jax.ShapeDtypeStruct((n * chunk_a, width), BF16),
            jax.ShapeDtypeStruct((n * chunk_b, width), BF16),
        ),
        in_specs=[smem] * 3 + [hbm] * 8,
        out_specs=(vmem,) * 3,
        scratch_shapes=[
            pltpu.VMEM((width, width), BF16),
            pltpu.VMEM((2 * width, width), BF16),
            pltpu.VMEM((1, width), F32),
            pltpu.VMEM((width, width), BF16),
            pltpu.VMEM((1, width), F32),
            dma((5,)),
            pltpu.VMEM((micros, rows, width), BF16),
            pltpu.VMEM(tile_weights.shape, BF16),
            pltpu.VMEM((micros, rows, width), BF16),
            pltpu.VMEM((blocks, size, width), BF16),
            pltpu.VMEM((micros, entries, size, width), BF16),
            pltpu.VMEM((micros, 2, sends, size, width), BF16),
            pltpu.VMEM((blocks, size, entries * size), BF16),
            pltpu.VMEM((entries * size, blocks * size), BF16),
            pltpu.VMEM((micros, rows, width), BF16),
            pltpu.VMEM((micros, rows, width), BF16),
            pltpu.VMEM((micros, rows, width), F32),
            pltpu.VMEM((micros, rows, 1), F32),
            pltpu.VMEM((micros, rows, width), F32),
            pltpu.VMEM((2, rows, width), F32),
            pltpu.VMEM((2, blocks, size, width), F32),
            pltpu.VMEM((rows, width), BF16),
            pltpu.VMEM((rows, width), BF16),
            pltpu.VMEM((rows, width), BF16),
            pltpu.VMEM((micros, 2, sends, size, width), BF16),
            pltpu.VMEM((micros, 2, sends, size, width), BF16),
            pltpu.VMEM((n * chunk_a, width), F32),
            pltpu.VMEM((n * chunk_b, width), F32),
            pltpu.VMEM((n * chunk_a, width), BF16),
            pltpu.VMEM((n - 1, chunk_a, width), BF16),
            pltpu.VMEM((n * chunk_b, width), BF16),
            pltpu.VMEM((n - 1, chunk_b, width), BF16),
            dma(()),
            dma((micros,)),
            dma(()),
            dma((micros, 2)),
            dma((micros, 2)),
            dma((micros, 2)),
            dma((micros, 2)),
            dma((micros, parts)),
            dma((micros, parts)),
        ]
        + [dma((n - 1,))] * 8,
        compiler_params=pltpu.CompilerParams(
            collective_id=0, has_side_effects=True, vmem_limit_bytes=40 * 1024 * 1024
        ),
    )(
        tile_source.T,
        tile_count,
        send_blocks[0],
        node_latents[0],
        cotangent,
        tile_weights,
        w_message[0],
        w_first[0],
        bias_first,
        w_second[0],
        norm_gain,
    )
    grads, message, first, bias, second, gain = pl.pallas_call(
        unpack,
        out_shape=(
            jax.ShapeDtypeStruct((micros, rows, width), BF16),
            jax.ShapeDtypeStruct((width, width), F32),
            jax.ShapeDtypeStruct((2 * width, width), F32),
            jax.ShapeDtypeStruct((1, width), F32),
            jax.ShapeDtypeStruct((width, width), F32),
            jax.ShapeDtypeStruct((1, width), F32),
        ),
        in_specs=[vmem, vmem, vmem],
        out_specs=(anywhere,) + (vmem,) * 5,
        scratch_shapes=[dma(())],
        compiler_params=pltpu.CompilerParams(vmem_limit_bytes=8 * 1024 * 1024),
    )(grads, packed_a, packed_b)
    return (grads[None], message[None], first[None], bias, second[None], gain)


def solution(mesh):
    return jax.shard_map(
        functools.partial(per_device, mesh.shape["dom"], mesh.shape["section"]),
        mesh=mesh,
        in_specs=(
            P("section", None, "dom", None),
            P(None, "dom", None),
            P("dom", None, None, None),
            P("dom", None),
            P("dom"),
            P("dom", None, None),
            P("section", None, None),
            P("section", None, None),
            P("section", None),
            P("section", None, None),
            P("section", None),
        ),
        out_specs=(
            P("section", None, "dom", None),
            P("section", None, None),
            P("section", None, None),
            P("section", None),
            P("section", None, None),
            P("section", None),
        ),
        check_vma=False,
    )
```

```python
import functools
import math

import jax
import jax.numpy as jnp
from jax import lax
from jax.experimental import pallas as pl
from jax.experimental.pallas import tpu as pltpu
from jax.sharding import PartitionSpec as P

epsilon = 1e-05
MESH = pl.DeviceIdType.MESH
F32 = jnp.float32
BF16 = jnp.bfloat16
parts = 1


def mm(a, b):
    return jnp.dot(a, b, preferred_element_type=F32)


def mm_nt(a, b):
    return lax.dot_general(a, b, (((1,), (1,)), ((), ())), preferred_element_type=F32)


def mm_tn(a, b):
    return lax.dot_general(a, b, (((0,), (0,)), ((), ())), preferred_element_type=F32)


def kernel(
    n,
    sections,
    chunks,
    normaliser,
    source_ref,
    count_ref,
    send_ref,
    latents_hbm,
    cotangent_ref,
    tiles_hbm,
    w_message_hbm,
    w_first_hbm,
    bias_hbm,
    w_second_hbm,
    gain_hbm,
    out_ref,
    gathered_a,
    gathered_b,
    w_message_ref,
    w_first_ref,
    bias_ref,
    w_second_ref,
    gain_ref,
    weight_sem,
    latents_ref,
    tiles_ref,
    incoming,
    messages,
    extended,
    outbox,
    dense,
    dense_t,
    aggregates,
    hiddens,
    normeds,
    inverses,
    factors,
    partial,
    grad_own,
    grad_outs,
    grad_befores,
    grad_aggregates,
    backbox,
    backs,
    totals,
    message_total,
    send_a,
    recv_a,
    send_b,
    recv_b,
    cot_sem,
    latents_sem,
    tiles_sem,
    out_send,
    out_recv,
    back_send,
    back_recv,
    sec_send,
    sec_recv,
    rs_send_a,
    rs_recv_a,
    ag_send_a,
    ag_recv_a,
    rs_send_b,
    rs_recv_b,
    ag_send_b,
    ag_recv_b,
):
    me = lax.axis_index("dom")
    section = lax.axis_index("section")
    is_last = section == sections - 1
    right, left = lax.rem(me + 1, n), lax.rem(me + n - 1, n)
    micros, rows, width = latents_ref.shape
    blocks, slots, size, _ = tiles_ref.shape
    entries = extended.shape[1]
    sends = (entries - blocks) // 2

    barrier = pltpu.get_barrier_semaphore()

    def greet(offset, carry):
        pl.semaphore_signal(
            barrier, inc=1, device_id=(lax.rem(me + offset, n), section), device_id_type=MESH
        )
        return carry

    lax.fori_loop(1, n, greet, 0)

    @pl.when(section > 0)
    def _():
        pl.semaphore_signal(barrier, inc=1, device_id=(me, section - 1), device_id_type=MESH)

    @pl.when(jnp.logical_not(is_last))
    def _():
        pl.semaphore_signal(barrier, inc=1, device_id=(me, section + 1), device_id_type=MESH)

    def latents_copy(m):
        return pltpu.make_async_copy(latents_hbm.at[m], latents_ref.at[m], latents_sem.at[m])

    message_copy = pltpu.make_async_copy(w_message_hbm, w_message_ref, weight_sem.at[0])
    weight_copies = [
        pltpu.make_async_copy(w_first_hbm, w_first_ref, weight_sem.at[1]),
        pltpu.make_async_copy(bias_hbm, bias_ref, weight_sem.at[2]),
        pltpu.make_async_copy(w_second_hbm, w_second_ref, weight_sem.at[3]),
        pltpu.make_async_copy(gain_hbm, gain_ref, weight_sem.at[4]),
    ]
    message_copy.start()
    for m in range(micros):
        latents_copy(m).start()
    for copy in weight_copies:
        copy.start()
    tiles_copy = pltpu.make_async_copy(tiles_hbm, tiles_ref, tiles_sem)
    tiles_copy.start()

    cot_copy = pltpu.make_async_copy(cotangent_ref, incoming, cot_sem)

    @pl.when(is_last)
    def _():
        cot_copy.start()

    def make_messages(m, carry):
        latents_copy(m).wait()
        value = mm(latents_ref[m], w_message_ref[...]).astype(BF16)
        value = value.reshape(blocks, size, width)
        extended[m, 0:blocks] = value
        messages[...] = value
        for side in range(2):
            for j in range(sends):
                outbox[m, side, j] = messages[send_ref[side, j]]
        return carry

    message_copy.wait()
    make_messages(0, 0)
    pl.semaphore_wait(
        barrier, n - 1 + jnp.where(section > 0, 1, 0) + jnp.where(is_last, 0, 1)
    )

    def halo_copy(m, side):
        start = blocks + (0 if side == 1 else sends)
        return pltpu.make_async_remote_copy(
            src_ref=outbox.at[m, side],
            dst_ref=extended.at[m, pl.ds(start, sends)],
            send_sem=out_send.at[m, side],
            recv_sem=out_recv.at[m, side],
            device_id=(right if side == 1 else left, section),
            device_id_type=MESH,
        )

    def back_copy(m, side):
        return pltpu.make_async_remote_copy(
            src_ref=backbox.at[m, side],
            dst_ref=backs.at[m, side],
            send_sem=back_send.at[m, side],
            recv_sem=back_recv.at[m, side],
            device_id=(left if side == 0 else right, section),
            device_id_type=MESH,
        )

    part_rows = rows // parts

    def section_copy(m, q):
        span = pl.ds(q * part_rows, part_rows)
        return pltpu.make_async_remote_copy(
            src_ref=out_ref.at[m, span],
            dst_ref=incoming.at[m, span],
            send_sem=sec_send.at[m, q],
            recv_sem=sec_recv.at[m, q],
            device_id=(me, section - 1),
            device_id_type=MESH,
        )

    def start_halo(m, carry):
        halo_copy(m, 0).start()
        halo_copy(m, 1).start()
        return carry

    start_halo(0, 0)
    lax.fori_loop(1, micros, make_messages, 0)
    start_halo(1, 0)
    for copy in weight_copies:
        copy.wait()
    tiles_copy.wait()

    def build(b, carry):
        live = [k < count_ref[b] for k in range(slots)]
        tiles = [tiles_ref[b, k].astype(F32) for k in range(slots)]
        flipped = [tile.T for tile in tiles]
        column = pl.ds(pl.multiple_of(b * size, size), size)
        for e in range(entries):
            value = jnp.zeros((size, size), F32)
            value_t = jnp.zeros((size, size), F32)
            for k in range(slots):
                hit = jnp.logical_and(source_ref[k, b] == e, live[k])
                weight = jnp.where(hit, 1.0, 0.0).astype(F32)
                value = value + tiles[k] * weight
                value_t = value_t + flipped[k] * weight
            dense[b, :, e * size : (e + 1) * size] = value.astype(BF16)
            dense_t[e * size : (e + 1) * size, column] = value_t.astype(BF16)
        return carry

    lax.fori_loop(0, blocks, build, 0)

    totals[...] = jnp.zeros_like(totals)
    message_total[...] = jnp.zeros_like(message_total)

    def forward(m):
        halo_copy(m, 0).wait_recv()
        halo_copy(m, 1).wait_recv()
        lax.fori_loop(jnp.minimum(m + 2, micros), jnp.minimum(m + 3, micros), start_halo, 0)
        coupling = dense[...].reshape(rows, entries * size)
        aggregate = mm(coupling, extended[m].reshape(entries * size, width)).astype(BF16)
        aggregates[m] = aggregate
        joined = jnp.concatenate([latents_ref[m], aggregate], axis=1)
        before = mm(joined, w_first_ref[...]) + bias_ref[...]
        sigmoid = 1.0 / (1.0 + jnp.exp(-before))
        hidden = (before * sigmoid).astype(BF16)
        hiddens[m] = hidden
        factors[m] = sigmoid * (1.0 + before * (1.0 - sigmoid))
        output = mm(hidden, w_second_ref[...])
        centred = output - jnp.mean(output, axis=-1, keepdims=True)
        inverse = lax.rsqrt(jnp.mean(centred * centred, axis=-1, keepdims=True) + epsilon)
        normeds[m] = centred * inverse
        inverses[m] = inverse

    def upfront(m, carry):
        forward(m)
        return carry

    @pl.when(is_last)
    def _():
        cot_copy.wait()

    def row_part(index, chunk):
        return pl.ds(pl.multiple_of(index * chunk, 16), chunk)

    def reduction(chunk, source, landing, result, sems):
        rs_send, rs_recv, ag_send, ag_recv = sems

        def rs_copy(offset):
            peer = lax.rem(me + offset, n)
            return pltpu.make_async_remote_copy(
                src_ref=source.at[row_part(peer, chunk)],
                dst_ref=landing.at[offset - 1],
                send_sem=rs_send.at[offset - 1],
                recv_sem=rs_recv.at[offset - 1],
                device_id=(peer, section),
                device_id_type=MESH,
            )

        def ag_copy(offset, owner):
            return pltpu.make_async_remote_copy(
                src_ref=result.at[row_part(owner, chunk)],
                dst_ref=result.at[row_part(owner, chunk)],
                send_sem=ag_send.at[offset - 1],
                recv_sem=ag_recv.at[offset - 1],
                device_id=(lax.rem(me + offset, n), section),
                device_id_type=MESH,
            )

        def each(body):
            def step(offset, carry):
                body(offset)
                return carry

            lax.fori_loop(1, n, step, 0)

        def scatter(total):
            source[...] = total[...].astype(BF16)
            each(lambda offset: rs_copy(offset).start())

        def gather(total):
            def collect(offset, value):
                rs_copy(offset).wait()
                return value + landing[offset - 1].astype(F32)

            value = lax.fori_loop(1, n, collect, total[row_part(me, chunk), :])
            result[row_part(me, chunk), :] = (value * normaliser).astype(BF16)
            each(lambda offset: ag_copy(offset, me).start())

        def finish():
            each(lambda offset: ag_copy(offset, lax.rem(me + n - offset, n)).wait_recv())
            each(lambda offset: ag_copy(offset, me).wait_send())

        return scatter, gather, finish

    scatter_a, gather_a, finish_a = reduction(
        chunks[0], send_a, recv_a, gathered_a, (rs_send_a, rs_recv_a, ag_send_a, ag_recv_a)
    )
    scatter_b, gather_b, finish_b = reduction(
        chunks[1], send_b, recv_b, gathered_b, (rs_send_b, rs_recv_b, ag_send_b, ag_recv_b)
    )

    def first_half(m, carry):
        slot = lax.rem(m, 2)
        gain_row = jnp.zeros((1, width), F32)
        bias_row = jnp.zeros((1, width), F32)
        for q in range(parts):
            span = slice(q * part_rows, (q + 1) * part_rows)

            @pl.when(jnp.logical_not(is_last))
            def _():
                section_copy(m, q).wait_recv()

            value = incoming[m, span].astype(F32)
            normed = normeds[m, span]
            gain_row += jnp.sum(value * normed, axis=0, keepdims=True)
            scaled = value * gain_ref[...]
            grad_out = inverses[m, span] * (
                scaled
                - jnp.mean(scaled, axis=-1, keepdims=True)
                - normed * jnp.mean(scaled * normed, axis=-1, keepdims=True)
            )
            grad_out = grad_out.astype(BF16)
            grad_outs[span] = grad_out
            grad_before = (mm_nt(grad_out, w_second_ref[...]) * factors[m, span]).astype(BF16)
            grad_befores[span] = grad_before
            bias_row += jnp.sum(grad_before.astype(F32), axis=0, keepdims=True)
            grad_joined = mm_nt(grad_before, w_first_ref[...])
            partial[slot, span] = value + grad_joined[:, :width]
            grad_aggregates[span] = grad_joined[:, width:].astype(BF16)
        for side in range(2):
            start = (blocks + side * sends) * size
            rim = mm(dense_t[start : start + sends * size, :], grad_aggregates[...])
            backbox[m, side] = rim.astype(BF16).reshape(sends, size, width)
            back_copy(m, side).start()
        own = mm(dense_t[: blocks * size, :], grad_aggregates[...])
        grad_own[slot] = own.reshape(blocks, size, width)
        joined = jnp.concatenate([latents_ref[m], aggregates[m]], axis=1)
        totals[: 2 * width] += mm_tn(joined, grad_befores[...])
        totals[2 * width : 3 * width] += mm_tn(hiddens[m], grad_outs[...])
        totals[3 * width : 3 * width + 1] += bias_row
        totals[3 * width + 1 : 3 * width + 2] += gain_row

        return carry

    def second_half(m, carry):
        slot = lax.rem(m, 2)
        back_copy(m, 0).wait_recv()
        back_copy(m, 1).wait_recv()
        for q in range(parts):
            span = slice(q * part_rows, (q + 1) * part_rows)
            pieces = []
            for i in range(q * blocks // parts, (q + 1) * blocks // parts):
                piece = grad_own[slot, i]
                for j in range(sends):
                    to_next = jnp.where(send_ref[1, j] == i, 1.0, 0.0).astype(F32)
                    to_previous = jnp.where(send_ref[0, j] == i, 1.0, 0.0).astype(F32)
                    piece = piece + backs[m, 0, j].astype(F32) * to_next
                    piece = piece + backs[m, 1, j].astype(F32) * to_previous
                pieces.append(piece.astype(BF16))
            grad_messages = jnp.concatenate(pieces, axis=0)
            grad_outs[span] = grad_messages
            result = partial[slot, span] + mm_nt(grad_messages, w_message_ref[...])
            out_ref[m, span] = result.astype(BF16)

            @pl.when(section > 0)
            def _():
                section_copy(m, q).start()

        message_total[0:width] += mm_tn(latents_ref[m], grad_outs[...])
        return carry

    def turn(t, carry):
        start = jnp.where(is_last, t, jnp.where(t == 0, 0, micros))
        stop = jnp.where(is_last, jnp.minimum(t + 1, micros), micros)
        lax.fori_loop(start, stop, upfront, 0)
        lax.fori_loop(t, jnp.minimum(t + 1, micros), first_half, 0)

        @pl.when(t == micros)
        def _():
            scatter_a(totals)

        lax.fori_loop(jnp.maximum(t - 1, 0), t, second_half, 0)
        return carry

    lax.fori_loop(0, micros + 1, turn, 0)
    scatter_b(message_total)
    gather_a(totals)
    gather_b(message_total)

    def finish_halos(m, carry):
        for side in range(2):
            halo_copy(m, side).wait_send()
            back_copy(m, side).wait_send()
        return carry

    lax.fori_loop(0, micros, finish_halos, 0)

    def finish_section(m, carry):
        for q in range(parts):
            section_copy(m, q).wait_send()
        return carry

    @pl.when(section > 0)
    def _():
        lax.fori_loop(0, micros, finish_section, 0)

    finish_a()
    finish_b()


def unpack(grads_ref, a_ref, b_ref, out_ref, message_ref, first_ref, bias_ref, second_ref, gain_ref, sem):
    width = message_ref.shape[-1]
    copy = pltpu.make_async_copy(grads_ref, out_ref, sem)
    copy.start()
    message_ref[...] = b_ref[0:width].astype(F32)
    first_ref[...] = a_ref[0 : 2 * width].astype(F32)
    second_ref[...] = a_ref[2 * width : 3 * width].astype(F32)
    tail = a_ref[3 * width : 3 * width + 16].astype(F32)
    bias_ref[...] = tail[0:1]
    gain_ref[...] = tail[1:2]
    copy.wait()


def per_device(
    n,
    sections,
    node_latents,
    cotangent,
    tile_weights,
    tile_source,
    tile_count,
    send_blocks,
    w_message,
    w_first,
    bias_first,
    w_second,
    norm_gain,
):
    micros, rows, width = cotangent.shape
    blocks, slots, size, _ = tile_weights.shape
    sends = send_blocks.shape[2]
    entries = blocks + 2 * sends
    chunk_a = -(-(3 * width + 16) // (16 * n)) * 16
    chunk_b = -(-width // (16 * n)) * 16
    normaliser = 1.0 / math.sqrt(micros * rows * n)
    vmem = pl.BlockSpec(memory_space=pltpu.VMEM)
    smem = pl.BlockSpec(memory_space=pltpu.SMEM)
    anywhere = pl.BlockSpec(memory_space=pl.ANY)
    hbm = pl.BlockSpec(memory_space=pltpu.HBM)
    dma = pltpu.SemaphoreType.DMA
    grads, packed_a, packed_b = pl.pallas_call(
        functools.partial(kernel, n, sections, (chunk_a, chunk_b), normaliser),
        out_shape=(
            jax.ShapeDtypeStruct((micros, rows, width), BF16),
            jax.ShapeDtypeStruct((n * chunk_a, width), BF16),
            jax.ShapeDtypeStruct((n * chunk_b, width), BF16),
        ),
        in_specs=[smem] * 3 + [hbm] * 8,
        out_specs=(vmem,) * 3,
        scratch_shapes=[
            pltpu.VMEM((width, width), BF16),
            pltpu.VMEM((2 * width, width), BF16),
            pltpu.VMEM((1, width), F32),
            pltpu.VMEM((width, width), BF16),
            pltpu.VMEM((1, width), F32),
            dma((5,)),
            pltpu.VMEM((micros, rows, width), BF16),
            pltpu.VMEM(tile_weights.shape, BF16),
            pltpu.VMEM((micros, rows, width), BF16),
            pltpu.VMEM((blocks, size, width), BF16),
            pltpu.VMEM((micros, entries, size, width), BF16),
            pltpu.VMEM((micros, 2, sends, size, width), BF16),
            pltpu.VMEM((blocks, size, entries * size), BF16),
            pltpu.VMEM((entries * size, blocks * size), BF16),
            pltpu.VMEM((micros, rows, width), BF16),
            pltpu.VMEM((micros, rows, width), BF16),
            pltpu.VMEM((micros, rows, width), F32),
            pltpu.VMEM((micros, rows, 1), F32),
            pltpu.VMEM((micros, rows, width), F32),
            pltpu.VMEM((2, rows, width), F32),
            pltpu.VMEM((2, blocks, size, width), F32),
            pltpu.VMEM((rows, width), BF16),
            pltpu.VMEM((rows, width), BF16),
            pltpu.VMEM((rows, width), BF16),
            pltpu.VMEM((micros, 2, sends, size, width), BF16),
            pltpu.VMEM((micros, 2, sends, size, width), BF16),
            pltpu.VMEM((n * chunk_a, width), F32),
            pltpu.VMEM((n * chunk_b, width), F32),
            pltpu.VMEM((n * chunk_a, width), BF16),
            pltpu.VMEM((n - 1, chunk_a, width), BF16),
            pltpu.VMEM((n * chunk_b, width), BF16),
            pltpu.VMEM((n - 1, chunk_b, width), BF16),
            dma(()),
            dma((micros,)),
            dma(()),
            dma((micros, 2)),
            dma((micros, 2)),
            dma((micros, 2)),
            dma((micros, 2)),
            dma((micros, parts)),
            dma((micros, parts)),
        ]
        + [dma((n - 1,))] * 8,
        compiler_params=pltpu.CompilerParams(
            collective_id=0, has_side_effects=True, vmem_limit_bytes=56 * 1024 * 1024
        ),
    )(
        tile_source.T,
        tile_count,
        send_blocks[0],
        node_latents[0],
        cotangent,
        tile_weights,
        w_message[0],
        w_first[0],
        bias_first,
        w_second[0],
        norm_gain,
    )
    grads, message, first, bias, second, gain = pl.pallas_call(
        unpack,
        out_shape=(
            jax.ShapeDtypeStruct((micros, rows, width), BF16),
            jax.ShapeDtypeStruct((width, width), F32),
            jax.ShapeDtypeStruct((2 * width, width), F32),
            jax.ShapeDtypeStruct((1, width), F32),
            jax.ShapeDtypeStruct((width, width), F32),
            jax.ShapeDtypeStruct((1, width), F32),
        ),
        in_specs=[vmem, vmem, vmem],
        out_specs=(anywhere,) + (vmem,) * 5,
        scratch_shapes=[dma(())],
    )(grads, packed_a, packed_b)
    return (grads[None], message[None], first[None], bias, second[None], gain)


def solution(mesh):
    return jax.shard_map(
        functools.partial(per_device, mesh.shape["dom"], mesh.shape["section"]),
        mesh=mesh,
        in_specs=(
            P("section", None, "dom", None),
            P(None, "dom", None),
            P("dom", None, None, None),
            P("dom", None),
            P("dom"),
            P("dom", None, None),
            P("section", None, None),
            P("section", None, None),
            P("section", None),
            P("section", None, None),
            P("section", None),
        ),
        out_specs=(
            P("section", None, "dom", None),
            P("section", None, None),
            P("section", None, None),
            P("section", None),
            P("section", None, None),
            P("section", None),
        ),
        check_vma=False,
    )
```
